32 devices in a mesh: slab: 4 (over y, x), energy: 8 (over z, core).
Axes of the slice: x: 2, y: 2, z: 4, core: 2. Of those that a mesh axis runs over, the one named last changes fastest.
Arguments:
- energies: float32 [8], P('energy'), may hold values from -1 to 1
- broadening: float32 [8], P('energy'), may hold values from 0.3 to 1
- hamiltonian: float32 [1024, 256], P('slab'), as said below
- coupling: float32 [1024, 256], P('slab'), may hold values from -0.21875 to 0.21875
- propagator: float32 [2, 6, 8, 8], replicated, may hold values from -2 to 2
- neighbors: int32 [1024, 32], P('slab'), may hold values from 0 to 255, as said below
- phonon_modes: int32 [1024, 32], P('slab'), may hold values from 0 to 5
Outputs:
- green_blocks: float32 [8, 2, 1024, 256], P('energy', None, 'slab')
- self_energy: float32 [8, 2, 32768], P('energy', None, 'slab')
The draws below stay inside these ranges and needn't reach their ends.
Inputs may be any that keep to these rules, and one draw needn't show every extreme that they name: `hamiltonian`: each block of 256 rows is symmetric. `neighbors`: an orbital is never its own neighbour.
All inputs are finite; a program needn't handle non-finite values.
Results may differ from the reference program's by a relative error of at most 0.0001.
Values sent between devices are 32-bit elements; how exact they have to be, the bound alone decides.
A program may use at most 128 MiB of HBM per device.

```python
import math
import jax
import jax.numpy as jnp
from jax import lax

B = 256
NEIGH = 32
MODES = 6
ENERGIES = 8
ORB = 1024


def draw_hamiltonian(key, part):
    key_site = jax.random.fold_in(key, 11)
    key_hop = jax.random.fold_in(key, 12)
    block_count = ORB // B
    spread = 0.3 / math.sqrt(B)
    hopping = jax.random.normal(key_hop, (block_count, B, B), jnp.float32) * spread
    hopping = jnp.clip(hopping, -6.0 * spread, 6.0 * spread)
    identity = jnp.eye(B, dtype=jnp.float32)
    symmetric = (hopping + jnp.swapaxes(hopping, 1, 2)) / math.sqrt(2.0) * (1.0 - identity)
    onsite = jax.random.uniform(key_site, (block_count, B), jnp.float32, -3.0, -2.0)
    return (symmetric + identity * onsite[:, :, None]).reshape(ORB, B)


def draw_neighbors(key, part):
    offsets = jax.random.randint(jax.random.fold_in(key, 21), (ORB, NEIGH), 1, B)
    positions = (jnp.arange(ORB, dtype=jnp.int32) % B)[:, None]
    return ((positions + offsets) % B).astype(jnp.int32)


def set_ends(array, rng, least, high):
    longest = array.shape.index(max(array.shape))
    spots = []
    for shift in (0, 1):
        where = [jax.random.randint(jax.random.fold_in(rng, axis), (), 0, length) for axis, length in enumerate(array.shape)]
        where[longest] = (where[longest] + shift) % array.shape[longest]
        spots.append(tuple(where))
    return array.at[spots[0]].set(least).at[spots[1]].set(high)


def shard_levels(rng, shape, cuts, least, top_value):
    loudness, own = 1.0, jax.random.fold_in(rng, 6)
    for position, parts in cuts:
        steps = jnp.exp(jax.random.uniform(jax.random.fold_in(own, position), (parts,), jnp.float32, least / len(cuts), top_value / len(cuts)))
        loudness = loudness * jnp.repeat(steps, shape[position] // parts).reshape([-1 if axis == position else 1 for axis in range(len(shape))])
    return loudness


def bell_draw(key, shape, deviation, most, shards=(), kind=jnp.bfloat16):
    result = jax.random.normal(key, shape, jnp.float32) * deviation
    if len(shards) > 0:
        result = shard_levels(key, shape, shards, -0.22, 0.18) * result
    return jnp.clip(result, min=-most, max=most).astype(kind)


def setup_inputs(seed: int = 0) -> dict:
    arg_keys = jax.random.split(jax.random.key(seed), 8)
    energies = jnp.clip(jax.random.uniform(arg_keys[0], (ENERGIES,), jnp.float32, -1.0, 1.0) * shard_levels(arg_keys[0], (ENERGIES,), ((0, 8),), -0.4, 0.0), -1.0, 1.0)
    broadening = jnp.clip(0.3 + 0.7 * jax.random.uniform(arg_keys[1], (ENERGIES,), jnp.float32) ** shard_levels(arg_keys[1], (ENERGIES,), ((0, 8),), -0.2, 0.2), 0.3, 1.0)
    hamiltonian = draw_hamiltonian(jax.random.fold_in(arg_keys[7], 71), 0)
    coupling = bell_draw(arg_keys[3], (ORB, B), (11 * B // 4) ** -0.5, 0.21875, ((0, 4),), jnp.float32)
    propagator = bell_draw(arg_keys[4], (2, MODES, ENERGIES, ENERGIES), ENERGIES ** -0.5, 2.0, (), jnp.float32)
    neighbors = draw_neighbors(jax.random.fold_in(arg_keys[7], 71), 0)
    phonon_modes = set_ends(jax.random.randint(arg_keys[6], (ORB, NEIGH), 0, MODES), jax.random.fold_in(arg_keys[6], 1), 0, MODES - 1).astype(jnp.int32)
    return dict(energies=energies, broadening=broadening, hamiltonian=hamiltonian, coupling=coupling, propagator=propagator, neighbors=neighbors, phonon_modes=phonon_modes)


HIGHEST = lax.Precision.HIGHEST

def complex_product(left, right):
    left_real, left_imag = (left[:, 0], left[:, 1])
    right_real, right_imag = (right[:, 0], right[:, 1])
    first = jnp.matmul(left_real, right_real, precision=HIGHEST)
    second = jnp.matmul(left_imag, right_imag, precision=HIGHEST)
    mixed = jnp.matmul(left_real + left_imag, right_real + right_imag, precision=HIGHEST)
    return jnp.stack([first - second, mixed - first - second], axis=1)

def newton_step(schur, inverse):
    identity = jnp.eye(schur.shape[-1], dtype=jnp.float32)
    residue = -complex_product(schur, inverse)
    residue = residue.at[:, 0].add(2.0 * identity)
    return complex_product(inverse, residue)

def jacobi_refine(schur):
    identity = jnp.eye(schur.shape[-1], dtype=jnp.float32)
    diagonal = jnp.diagonal(schur, axis1=2, axis2=3)
    diag_real, diag_imag = (diagonal[:, 0], diagonal[:, 1])
    modulus = diag_real * diag_real + diag_imag * diag_imag
    inv_real = diag_real / modulus
    inv_imag = -diag_imag / modulus
    outer_real = inv_real[:, :, None] * inv_real[:, None, :] - inv_imag[:, :, None] * inv_imag[:, None, :]
    outer_imag = inv_real[:, :, None] * inv_imag[:, None, :] + inv_imag[:, :, None] * inv_real[:, None, :]
    schur_real, schur_imag = (schur[:, 0], schur[:, 1])
    first_real = 2.0 * identity * inv_real[:, :, None] - (outer_real * schur_real - outer_imag * schur_imag)
    first_imag = 2.0 * identity * inv_imag[:, :, None] - (outer_real * schur_imag + outer_imag * schur_real)
    first_iterate = jnp.stack([first_real, first_imag], axis=1)
    return newton_step(schur, first_iterate)

def convolve_modes(kernel, values, one_hot):
    spread = one_hot[:, None, None, :] * values[None]
    real_part = jnp.einsum('mef,mfp->ep', kernel[0], spread[:, :, 0], precision=HIGHEST) - jnp.einsum('mef,mfp->ep', kernel[1], spread[:, :, 1], precision=HIGHEST)
    imag_part = jnp.einsum('mef,mfp->ep', kernel[0], spread[:, :, 1], precision=HIGHEST) + jnp.einsum('mef,mfp->ep', kernel[1], spread[:, :, 0], precision=HIGHEST)
    return jnp.stack([real_part, imag_part], axis=1)

def dense_sigma(self_part, block_neighbors):
    orbitals = block_neighbors.shape[0]
    reshaped = self_part.reshape(self_part.shape[0], 2, orbitals, block_neighbors.shape[1])
    row_index = jnp.broadcast_to(jnp.arange(orbitals, dtype=jnp.int32)[:, None], block_neighbors.shape)
    empty = jnp.zeros((self_part.shape[0], 2, orbitals, orbitals), jnp.float32)
    return empty.at[:, :, row_index, block_neighbors].add(reshaped)

def reference(energies, broadening, hamiltonian, coupling, propagator, neighbors, phonon_modes):
    coupling_scale = 2.0 * math.sqrt(B / NEIGH)
    identity = jnp.eye(B, dtype=jnp.float32)
    block_count = ORB // B
    previous = jnp.zeros((ENERGIES, 2, B, B), jnp.float32)
    schurs = []
    inverses = []
    for block in range(block_count):
        rows = slice(block * B, (block + 1) * B)
        block_ham = hamiltonian[rows]
        block_cpl = coupling[rows]
        shifted = jnp.stack([energies[:, None, None] * identity - block_ham[None], broadening[:, None, None] * identity + jnp.zeros_like(block_ham)[None]], axis=1)
        through = jnp.matmul(jnp.matmul(block_cpl, previous, precision=HIGHEST), block_cpl.T, precision=HIGHEST)
        schur = shifted - through
        inverse = jacobi_refine(schur)
        schurs.append(schur)
        inverses.append(inverse)
        previous = inverse
    greens = []
    selves = []
    mode_ids = jnp.arange(MODES, dtype=jnp.int32)
    for block in range(block_count):
        rows = slice(block * B, (block + 1) * B)
        block_nbr = neighbors[rows]
        inverse = inverses[block]
        index = jnp.broadcast_to(block_nbr, inverse.shape[:2] + block_nbr.shape)
        pair_green = jnp.take_along_axis(inverse, index, axis=3).reshape(ENERGIES, 2, B * NEIGH)
        modes_flat = phonon_modes[rows].reshape(-1)
        one_hot = (modes_flat[None, :] == mode_ids[:, None]).astype(jnp.float32)
        self_part = coupling_scale * convolve_modes(propagator, pair_green, one_hot)
        sigma = dense_sigma(self_part, block_nbr)
        residue = -complex_product(schurs[block] - sigma, inverse)
        residue = residue.at[:, 0].add(2.0 * identity)
        greens.append(complex_product(inverse, residue))
        selves.append(self_part)
    return (jnp.concatenate(greens, axis=2), jnp.concatenate(selves, axis=2))
```

```python
import functools
import math

import jax
import jax.numpy as jnp
from jax import lax
from jax.experimental import pallas as pl
from jax.experimental.pallas import tpu as pltpu
from jax.sharding import PartitionSpec as P

F32 = jnp.float32
BF16 = jnp.bfloat16
MESH = pl.DeviceIdType.MESH
LANES = 128


def split(x):
    hi = x.astype(BF16)
    return hi, (x - hi.astype(F32)).astype(BF16)


def dot3(a, b, transposed=False):
    dims = (((1,), (1 if transposed else 0,)), ((), ()))
    dot = functools.partial(lax.dot_general, dimension_numbers=dims, preferred_element_type=F32)
    return dot(a[0], b[0]) + (dot(a[0], b[1]) + dot(a[1], b[0]))


def triple(re, im):
    return split(re), split(im), split(re + im)


def product(a, b):
    first, second, mixed = (dot3(x, y) for x, y in zip(a, b))
    return first - second, mixed - first - second


def take(values, index):
    return jnp.take_along_axis(values, index, axis=1, mode="promise_in_bounds")


def kernel(
    slabs, points, scale,
    en_ref, br_ref, h_ref, c_ref, k_ref, nbr_ref, mode_ref,
    green_ref, self_ref,
    hc, pg, s_ref, g_ref, rep, irep, inv_ref,
    send1, recv1, fwd1, send2, recv2, fwd2, twin_send,
):
    size = h_ref.shape[0]
    listed = nbr_ref.shape[1]
    modes = k_ref.shape[1]
    groups = LANES // listed
    packed_rows = size // groups
    chunks = size // LANES
    chips = points // 2
    me_slab, me = lax.axis_index("slab"), lax.axis_index("energy")
    par, chip = lax.rem(me, 2), lax.div(me, 2)
    twin = me + 1 - 2 * par

    barrier = pltpu.get_barrier_semaphore()

    def greet(slab, point):
        pl.semaphore_signal(barrier, inc=1, device_id=(slab, point), device_id_type=MESH)

    for d in range(1, slabs):
        greet(lax.rem(me_slab + d, slabs), me)
    greet(me_slab, twin)
    for d in range(1, chips):
        greet(me_slab, lax.rem(chip + d, chips) * 2 + par)
    pl.semaphore_wait(barrier, slabs - 1 + 1 + chips - 1)

    half_rows = size // 2

    def half(which):
        return pl.ds(pl.multiple_of(which * half_rows, half_rows), half_rows)

    def block_copy(target, item):
        return pltpu.make_async_remote_copy(
            src_ref=(h_ref, c_ref)[item].at[half(par)],
            dst_ref=hc.at[me_slab, item, half(par)],
            send_sem=send1.at[target, item],
            recv_sem=recv1.at[me_slab, item, par],
            device_id=(target, me),
            device_id_type=MESH,
        )

    def block_forward(b, item, which):
        place = hc.at[b, item, half(which)]
        return pltpu.make_async_remote_copy(
            src_ref=place, dst_ref=place,
            send_sem=fwd1.at[b, item], recv_sem=recv1.at[b, item, which],
            device_id=(me_slab, twin), device_id_type=MESH,
        )

    for target in reversed(range(1, slabs)):
        @pl.when(target > me_slab)
        def _():
            block_copy(target, 0).start()

            @pl.when(me_slab > 0)
            def _():
                block_copy(target, 1).start()

    hc[me_slab, 0] = h_ref[...]
    hc[me_slab, 1] = c_ref[...]

    row = lax.broadcasted_iota(jnp.int32, (size, size), 0)
    col = lax.broadcasted_iota(jnp.int32, (size, size), 1)
    eye = row == col

    column = lax.broadcasted_iota(jnp.int32, (size, size), 1)
    inv = jnp.full((size, size), -1, jnp.int32)
    for k in range(listed):
        inv = jnp.where(nbr_ref[:, k : k + 1] == column, k, inv)
    inv_ref[...] = inv

    group = lax.broadcasted_iota(jnp.int32, (packed_rows, LANES), 1) // listed

    def pack(ref):
        out = ref[pl.ds(0, packed_rows, stride=groups), :]
        for q in range(1, groups):
            out = jnp.where(group == q, ref[pl.ds(q, packed_rows, stride=groups), :], out)
        return out

    irep[0] = jnp.concatenate([nbr_ref[...]] * groups, axis=1)
    irep[1] = jnp.concatenate([mode_ref[...]] * groups, axis=1)

    def refine(b, through):
        s_re = jnp.where(eye, en_ref[0], 0.0) - hc[b, 0]
        s_im = jnp.where(eye, br_ref[0], 0.0)
        if through is not None:
            s_re, s_im = s_re - through[0], s_im - through[1]
        s_ref[0] = s_re
        s_ref[1] = s_im
        diag_re = jnp.where(eye, s_re, 0.0)
        diag_im = jnp.where(eye, s_im, 0.0)

        def reciprocal(axis):
            re = jnp.sum(diag_re, axis=axis, keepdims=True)
            im = jnp.sum(diag_im, axis=axis, keepdims=True)
            modulus = re * re + im * im
            return re / modulus, -im / modulus

        di_re, di_im = reciprocal(1)
        dj_re, dj_im = reciprocal(0)
        o_re = di_re * dj_re - di_im * dj_im
        o_im = di_re * dj_im + di_im * dj_re
        x_re = jnp.where(eye, 2.0 * di_re, 0.0) - (o_re * s_re - o_im * s_im)
        x_im = jnp.where(eye, 2.0 * di_im, 0.0) - (o_re * s_im + o_im * s_re)
        x = triple(x_re, x_im)
        p_re, p_im = product(triple(s_re, s_im), x)
        out_re, out_im = product(x, triple(jnp.where(eye, 2.0, 0.0) - p_re, -p_im))
        g_ref[0] = out_re
        g_ref[1] = out_im

    def arrive(b, items):
        @pl.when(b < me_slab)
        def _():
            for item in items:
                copy = block_forward(b, item, par)
                copy.wait_recv()
                copy.start()
            for item in items:
                block_forward(b, item, 1 - par).wait_recv()

    arrive(0, (0,))
    refine(0, None)

    def step(b, carry):
        arrive(b, (0, 1))
        c = split(hc[b, 1])
        through = [dot3(split(dot3(c, split(g_ref[i]))), c, transposed=True) for i in range(2)]
        refine(b, through)
        return carry

    lax.fori_loop(1, me_slab + 1, step, 0)

    for i in range(2):
        index = irep[0]
        values = take(g_ref[i, :, :LANES], index & (LANES - 1))
        for chunk in range(1, chunks):
            part = take(g_ref[i, :, chunk * LANES : (chunk + 1) * LANES], index & (LANES - 1))
            values = jnp.where(index >= chunk * LANES, part, values)
        rep[i] = values
        pg[me, i] = pack(rep.at[i])

    def pair_copy(d):
        other = lax.rem(chip + d, chips)
        return pltpu.make_async_remote_copy(
            src_ref=pg.at[me], dst_ref=pg.at[me],
            send_sem=send2.at[d], recv_sem=recv2.at[me],
            device_id=(me_slab, other * 2 + par), device_id_type=MESH,
        )

    def pair_forward(d, which):
        point = lax.rem(chip + d, chips) * 2 + which
        return pltpu.make_async_remote_copy(
            src_ref=pg.at[point], dst_ref=pg.at[point],
            send_sem=fwd2.at[d], recv_sem=recv2.at[point],
            device_id=(me_slab, twin), device_id_type=MESH,
        )

    def own_forward(point):
        return pltpu.make_async_remote_copy(
            src_ref=pg.at[point], dst_ref=pg.at[point],
            send_sem=twin_send, recv_sem=recv2.at[point],
            device_id=(me_slab, twin), device_id_type=MESH,
        )

    def each(first, last, act):
        lax.fori_loop(first, last, lambda d, carry: (act(d), carry)[1], 0)

    each(1, chips, lambda d: pair_copy(d).start())
    own_forward(me).start()

    g = triple(g_ref[0], g_ref[1])
    p_re, p_im = product(triple(s_ref[0], s_ref[1]), g)
    e_re, e_im = product(g, triple(jnp.where(eye, 2.0, 0.0) - p_re, -p_im))
    green_ref[0, 0] = e_re
    green_ref[0, 1] = e_im

    mode = pack(irep.at[1])
    nbr = pack(irep.at[0])

    def add_point(point, total):
        k_re = jnp.zeros((packed_rows, LANES), F32)
        k_im = jnp.zeros((packed_rows, LANES), F32)
        for m in range(modes):
            k_re = jnp.where(mode == m, k_ref[0, m, me, point], k_re)
            k_im = jnp.where(mode == m, k_ref[1, m, me, point], k_im)
        v_re, v_im = pg[point, 0], pg[point, 1]
        return total[0] + (k_re * v_re - k_im * v_im), total[1] + (k_re * v_im + k_im * v_re)

    zero = jnp.zeros((packed_rows, LANES), F32)
    total = add_point(me, (zero, zero))
    own_forward(twin).wait_recv()
    total = add_point(twin, total)

    def near(d, total):
        copy = pair_forward(d, par)
        copy.wait_recv()
        copy.start()
        return add_point(lax.rem(chip + d, chips) * 2 + par, total)

    def far(d, total):
        pair_forward(d, 1 - par).wait_recv()
        return add_point(lax.rem(chip + d, chips) * 2 + 1 - par, total)

    total = lax.fori_loop(1, chips, near, total)
    total = lax.fori_loop(1, chips, far, total)
    part = [scale * t for t in total]
    self_ref[0] = part[0]
    self_ref[1] = part[1]

    lane = lax.broadcasted_iota(jnp.int32, (packed_rows, LANES), 1)
    start = lane - lax.rem(lane, listed)
    summed = list(part)
    for d in range(1, listed):
        index = start + lax.rem(lane + d, listed)
        same = take(nbr, index) == nbr
        for i in range(2):
            summed[i] = summed[i] + jnp.where(same, take(part[i], index), 0.0)
    offset = lax.rem(lax.broadcasted_iota(jnp.int32, (size, LANES), 0), groups) * listed
    sigma = []
    for i in range(2):
        for q in range(groups):
            rep[i, pl.ds(q, packed_rows, stride=groups), :] = summed[i]
        values = rep[i]
        pieces = []
        for chunk in range(chunks):
            where = inv_ref[:, chunk * LANES : (chunk + 1) * LANES]
            pieces.append(
                jnp.where(where >= 0, take(values, offset + jnp.maximum(where, 0)), 0.0)
            )
        sigma.append(jnp.concatenate(pieces, axis=1))
    g = triple(g_ref[0], g_ref[1])
    p_re, p_im = product(triple(*sigma), g)
    f_re, f_im = product(g, triple(p_re, p_im))
    green_ref[0, 0] = green_ref[0, 0] + f_re
    green_ref[0, 1] = green_ref[0, 1] + f_im

    for target in range(1, slabs):
        @pl.when(target > me_slab)
        def _():
            block_copy(target, 0).wait_send()

            @pl.when(me_slab > 0)
            def _():
                block_copy(target, 1).wait_send()

    for b in range(slabs):
        @pl.when(b < me_slab)
        def _():
            for item in ((0,) if b == 0 else (0, 1)):
                block_forward(b, item, par).wait_send()

    each(1, chips, lambda d: pair_copy(d).wait_send())
    each(1, chips, lambda d: pair_forward(d, par).wait_send())
    own_forward(me).wait_send()


def body(slabs, points, energies, broadening, hamiltonian, coupling, propagator, neighbors, phonon_modes):
    assert energies.shape[0] == 1 and points % 2 == 0
    size, listed = neighbors.shape
    scale = 2.0 * math.sqrt(size / listed)
    packed = size * listed // LANES
    smem = pl.BlockSpec(memory_space=pltpu.SMEM)
    vmem = pl.BlockSpec(memory_space=pltpu.VMEM)
    dma = pltpu.SemaphoreType.DMA
    green, part = pl.pallas_call(
        functools.partial(kernel, slabs, points, scale),
        out_shape=(
            jax.ShapeDtypeStruct((1, 2, size, size), F32),
            jax.ShapeDtypeStruct((2, packed, LANES), F32),
        ),
        in_specs=[smem, smem, vmem, vmem, smem, vmem, vmem],
        out_specs=(vmem, vmem),
        scratch_shapes=[
            pltpu.VMEM((slabs, 2, size, size), F32),
            pltpu.VMEM((points, 2, packed, LANES), F32),
            pltpu.VMEM((2, size, size), F32),
            pltpu.VMEM((2, size, size), F32),
            pltpu.VMEM((2, size, LANES), F32),
            pltpu.VMEM((2, size, LANES), jnp.int32),
            pltpu.VMEM((size, size), jnp.int32),
            dma((slabs, 2)),
            dma((slabs, 2, 2)),
            dma((slabs, 2)),
            dma((points // 2,)),
            dma((points,)),
            dma((points // 2,)),
            dma,
        ],
        compiler_params=pltpu.CompilerParams(
            collective_id=0, has_side_effects=True, vmem_limit_bytes=40 * 1024 * 1024
        ),
        cost_estimate=pl.CostEstimate(
            flops=200 * size**3, bytes_accessed=8 * size * size * 4, transcendentals=0
        ),
    )(energies, broadening, hamiltonian, coupling, propagator, neighbors, phonon_modes)
    return green, part.reshape(1, 2, size * listed)


def solution(mesh):
    return jax.shard_map(
        functools.partial(body, mesh.shape["slab"], mesh.shape["energy"]),
        mesh=mesh,
        in_specs=(
            P("energy"),
            P("energy"),
            P("slab", None),
            P("slab", None),
            P(),
            P("slab", None),
            P("slab", None),
        ),
        out_specs=(P("energy", None, "slab", None), P("energy", None, "slab")),
        check_vma=False,
    )
```

```python
import functools
import math

import jax
import jax.numpy as jnp
from jax import lax
from jax.experimental import pallas as pl
from jax.experimental.pallas import tpu as pltpu
from jax.sharding import PartitionSpec as P

F32 = jnp.float32
BF16 = jnp.bfloat16
MESH = pl.DeviceIdType.MESH
LANES = 128


def split(x):
    hi = x.astype(BF16)
    return hi, (x - hi.astype(F32)).astype(BF16)


def dot3(a, b, transposed=False):
    dims = (((1,), (1 if transposed else 0,)), ((), ()))
    dot = functools.partial(lax.dot_general, dimension_numbers=dims, preferred_element_type=F32)
    return dot(a[0], b[0]) + (dot(a[0], b[1]) + dot(a[1], b[0]))


def triple(re, im):
    return split(re), split(im), split(re + im)


def product(a, b):
    first, second, mixed = (dot3(x, y) for x, y in zip(a, b))
    return first - second, mixed - first - second


def take(values, index):
    return jnp.take_along_axis(values, index, axis=1, mode="promise_in_bounds")


def kernel(
    slabs, points, scale,
    shift_ref, h_hbm, c_hbm, k_hbm, nbr_hbm, mode_hbm,
    green_ref, self_ref,
    h_ref, hp, cb, pg, s_ref, g_ref, rep, irep, inv_ref, lists, k_ref,
    local, send1, recv1, fwd1, send2, recv2, fwd2, twin_send,
):
    size = h_ref.shape[0]
    listed = nbr_hbm.shape[0]
    modes = k_ref.shape[1]
    groups = LANES // listed
    packed_rows = size // groups
    chunks = size // LANES
    chips = points // 2
    me_slab, me = lax.axis_index("slab"), lax.axis_index("energy")
    par, chip = lax.rem(me, 2), lax.div(me, 2)
    twin = me + 1 - 2 * par

    loads = [
        pltpu.make_async_copy(source, target, local.at[n])
        for n, (source, target) in enumerate(
            (
                (h_hbm, h_ref),
                (nbr_hbm, lists.at[0]),
                (mode_hbm, lists.at[1]),
                (c_hbm, cb.at[me_slab]),
                (k_hbm, k_ref),
            )
        )
    ]
    for load in loads:
        load.start()

    barrier = pltpu.get_barrier_semaphore()

    def greet(slab, point):
        pl.semaphore_signal(barrier, inc=1, device_id=(slab, point), device_id_type=MESH)

    for d in range(1, slabs):
        greet(lax.rem(me_slab + d, slabs), me)
    greet(me_slab, twin)
    for d in range(1, chips):
        greet(me_slab, lax.rem(chip + d, chips) * 2 + par)
    half_rows = size // 2

    def half(which):
        return pl.ds(pl.multiple_of(which * half_rows, half_rows), half_rows)

    def place(b, item, which):
        return hp.at[b, which] if item == 0 else cb.at[b, half(which)]

    def block_copy(target, item):
        return pltpu.make_async_remote_copy(
            src_ref=hp.at[me_slab, par] if item == 0 else c_hbm.at[half(par)],
            dst_ref=place(me_slab, item, par),
            send_sem=send1.at[target, item],
            recv_sem=recv1.at[me_slab, item, par],
            device_id=(target, me),
            device_id_type=MESH,
        )

    def block_forward(b, item, which):
        return pltpu.make_async_remote_copy(
            src_ref=place(b, item, which), dst_ref=place(b, item, which),
            send_sem=fwd1.at[b, item], recv_sem=recv1.at[b, item, which],
            device_id=(me_slab, twin), device_id_type=MESH,
        )

    small_row = lax.broadcasted_iota(jnp.int32, (half_rows, half_rows), 0)
    small_col = lax.broadcasted_iota(jnp.int32, (half_rows, half_rows), 1)
    loads[0].wait()
    first = h_ref[:half_rows, :half_rows]
    last = h_ref[half_rows:, half_rows:]
    hp[me_slab, 0, :half_rows] = jnp.where(small_row <= small_col, first, last)
    ends = jnp.sum(jnp.where(small_row == small_col, last, 0.0), axis=0, keepdims=True)
    hp[me_slab, 0, half_rows:] = jnp.broadcast_to(ends, (8, half_rows))
    hp[me_slab, 1, :half_rows] = h_ref[:half_rows, half_rows:]
    hp[me_slab, 1, half_rows:] = jnp.zeros((8, half_rows), F32)

    pl.semaphore_wait(barrier, slabs - 1 + 1 + chips - 1)

    for target in reversed(range(1, slabs)):
        @pl.when(target > me_slab)
        def _():
            block_copy(target, 0).start()

    for target in reversed(range(1, slabs)):
        @pl.when(jnp.logical_and(target > me_slab, me_slab > 0))
        def _():
            block_copy(target, 1).start()

    def hamiltonian_block(b):
        square = hp[b, 0, :half_rows]
        turned = square.T
        corner = hp[b, 1, :half_rows]
        ends = hp[b, 0, half_rows : half_rows + 1]
        first = jnp.where(small_row <= small_col, square, turned)
        last = jnp.where(small_row > small_col, square, turned)
        last = jnp.where(small_row == small_col, ends, last)
        top = jnp.concatenate([first, corner], axis=1)
        bottom = jnp.concatenate([corner.T, last], axis=1)
        return jnp.concatenate([top, bottom], axis=0)

    for load in loads[1:]:
        load.wait()

    row = lax.broadcasted_iota(jnp.int32, (size, size), 0)
    col = lax.broadcasted_iota(jnp.int32, (size, size), 1)
    eye = row == col

    irep[0] = jnp.concatenate([lists[0].T] * groups, axis=1)
    irep[1] = jnp.concatenate([lists[1].T] * groups, axis=1)

    column = lax.broadcasted_iota(jnp.int32, (size, size), 1)
    inv = jnp.full((size, size), -1, jnp.int32)
    for k in range(listed):
        inv = jnp.where(irep[0, :, k : k + 1] == column, k, inv)
    inv_ref[...] = inv

    group = lax.broadcasted_iota(jnp.int32, (packed_rows, LANES), 1) // listed

    def pack(ref):
        out = ref[pl.ds(0, packed_rows, stride=groups), :]
        for q in range(1, groups):
            out = jnp.where(group == q, ref[pl.ds(q, packed_rows, stride=groups), :], out)
        return out

    def refine(b, through):
        s_re = jnp.where(eye, shift_ref[:, :1], 0.0) - hamiltonian_block(b)
        s_im = jnp.where(eye, shift_ref[:, 1:], 0.0)
        if through is not None:
            s_re, s_im = s_re - through[0], s_im - through[1]
        s_ref[0] = s_re
        s_ref[1] = s_im
        diag_re = jnp.where(eye, s_re, 0.0)
        diag_im = jnp.where(eye, s_im, 0.0)

        def reciprocal(axis):
            re = jnp.sum(diag_re, axis=axis, keepdims=True)
            im = jnp.sum(diag_im, axis=axis, keepdims=True)
            modulus = re * re + im * im
            return re / modulus, -im / modulus

        di_re, di_im = reciprocal(1)
        dj_re, dj_im = reciprocal(0)
        o_re = di_re * dj_re - di_im * dj_im
        o_im = di_re * dj_im + di_im * dj_re
        x_re = jnp.where(eye, 2.0 * di_re, 0.0) - (o_re * s_re - o_im * s_im)
        x_im = jnp.where(eye, 2.0 * di_im, 0.0) - (o_re * s_im + o_im * s_re)
        x = triple(x_re, x_im)
        p_re, p_im = product(triple(s_re, s_im), x)
        out_re, out_im = product(x, triple(jnp.where(eye, 2.0, 0.0) - p_re, -p_im))
        g_ref[0] = out_re
        g_ref[1] = out_im

    def arrive(b, items):
        @pl.when(b < me_slab)
        def _():
            for item in items:
                copy = block_forward(b, item, par)
                copy.wait_recv()
                copy.start()
            for item in items:
                block_forward(b, item, 1 - par).wait_recv()

    arrive(0, (0,))
    refine(0, None)

    def step(b, carry):
        arrive(b, (0, 1))
        c = split(cb[b])
        through = [dot3(split(dot3(c, split(g_ref[i]))), c, transposed=True) for i in range(2)]
        refine(b, through)
        return carry

    lax.fori_loop(1, me_slab + 1, step, 0)

    for i in range(2):
        index = irep[0]
        values = take(g_ref[i, :, :LANES], index & (LANES - 1))
        for chunk in range(1, chunks):
            part = take(g_ref[i, :, chunk * LANES : (chunk + 1) * LANES], index & (LANES - 1))
            values = jnp.where(index >= chunk * LANES, part, values)
        rep[i] = values
        pg[me, i] = pack(rep.at[i])

    def pair_copy(d):
        other = lax.rem(chip + d, chips)
        return pltpu.make_async_remote_copy(
            src_ref=pg.at[me], dst_ref=pg.at[me],
            send_sem=send2.at[d], recv_sem=recv2.at[me],
            device_id=(me_slab, other * 2 + par), device_id_type=MESH,
        )

    def pair_forward(d, which):
        point = lax.rem(chip + d, chips) * 2 + which
        return pltpu.make_async_remote_copy(
            src_ref=pg.at[point], dst_ref=pg.at[point],
            send_sem=fwd2.at[d], recv_sem=recv2.at[point],
            device_id=(me_slab, twin), device_id_type=MESH,
        )

    def own_forward(point):
        return pltpu.make_async_remote_copy(
            src_ref=pg.at[point], dst_ref=pg.at[point],
            send_sem=twin_send, recv_sem=recv2.at[point],
            device_id=(me_slab, twin), device_id_type=MESH,
        )

    def each(first, last, act):
        lax.fori_loop(first, last, lambda d, carry: (act(d), carry)[1], 0)

    each(1, chips, lambda d: pair_copy(d).start())
    own_forward(me).start()

    g = triple(g_ref[0], g_ref[1])
    p_re, p_im = product(triple(s_ref[0], s_ref[1]), g)
    e_re, e_im = product(g, triple(jnp.where(eye, 2.0, 0.0) - p_re, -p_im))
    green_ref[0, 0] = e_re
    green_ref[0, 1] = e_im

    mode = pack(irep.at[1])
    nbr = pack(irep.at[0])

    def add_point(point, total):
        k_re = jnp.zeros((packed_rows, LANES), F32)
        k_im = jnp.zeros((packed_rows, LANES), F32)
        for m in range(modes):
            k_re = jnp.where(mode == m, k_ref[0, m, me, point], k_re)
            k_im = jnp.where(mode == m, k_ref[1, m, me, point], k_im)
        v_re, v_im = pg[point, 0], pg[point, 1]
        return total[0] + (k_re * v_re - k_im * v_im), total[1] + (k_re * v_im + k_im * v_re)

    zero = jnp.zeros((packed_rows, LANES), F32)
    total = add_point(me, (zero, zero))
    own_forward(twin).wait_recv()
    total = add_point(twin, total)

    def near(d, total):
        copy = pair_forward(d, par)
        copy.wait_recv()
        copy.start()
        return add_point(lax.rem(chip + d, chips) * 2 + par, total)

    def far(d, total):
        pair_forward(d, 1 - par).wait_recv()
        return add_point(lax.rem(chip + d, chips) * 2 + 1 - par, total)

    total = lax.fori_loop(1, chips, near, total)
    total = lax.fori_loop(1, chips, far, total)
    part = [scale * t for t in total]
    for line in range(packed_rows):
        self_ref[0, :, line * LANES : (line + 1) * LANES] = jnp.concatenate(
            [p[line : line + 1] for p in part], axis=0
        )

    lane = lax.broadcasted_iota(jnp.int32, (packed_rows, LANES), 1)
    start = lane - lax.rem(lane, listed)
    summed = list(part)
    for d in range(1, listed):
        index = start + lax.rem(lane + d, listed)
        same = take(nbr, index) == nbr
        for i in range(2):
            summed[i] = summed[i] + jnp.where(same, take(part[i], index), 0.0)
    offset = lax.rem(lax.broadcasted_iota(jnp.int32, (size, LANES), 0), groups) * listed
    sigma = []
    for i in range(2):
        for q in range(groups):
            rep[i, pl.ds(q, packed_rows, stride=groups), :] = summed[i]
        values = rep[i]
        pieces = []
        for chunk in range(chunks):
            where = inv_ref[:, chunk * LANES : (chunk + 1) * LANES]
            pieces.append(
                jnp.where(where >= 0, take(values, offset + jnp.maximum(where, 0)), 0.0)
            )
        sigma.append(jnp.concatenate(pieces, axis=1))
    g = triple(g_ref[0], g_ref[1])
    p_re, p_im = product(triple(*sigma), g)
    f_re, f_im = product(g, triple(p_re, p_im))
    green_ref[0, 0] = green_ref[0, 0] + f_re
    green_ref[0, 1] = green_ref[0, 1] + f_im

    for target in range(1, slabs):
        @pl.when(target > me_slab)
        def _():
            block_copy(target, 0).wait_send()

            @pl.when(me_slab > 0)
            def _():
                block_copy(target, 1).wait_send()

    for b in range(slabs):
        @pl.when(b < me_slab)
        def _():
            for item in ((0,) if b == 0 else (0, 1)):
                block_forward(b, item, par).wait_send()

    each(1, chips, lambda d: pair_copy(d).wait_send())
    each(1, chips, lambda d: pair_forward(d, par).wait_send())
    own_forward(me).wait_send()


def body(slabs, points, energies, broadening, hamiltonian, coupling, propagator, neighbors, phonon_modes):
    assert energies.shape[0] == 1 and points % 2 == 0
    size, listed = neighbors.shape
    scale = 2.0 * math.sqrt(size / listed)
    packed = size * listed // LANES
    hbm = pl.BlockSpec(memory_space=pltpu.HBM)
    vmem = pl.BlockSpec(memory_space=pltpu.VMEM)
    dma = pltpu.SemaphoreType.DMA
    green, part = pl.pallas_call(
        functools.partial(kernel, slabs, points, scale),
        out_shape=(
            jax.ShapeDtypeStruct((1, 2, size, size), F32),
            jax.ShapeDtypeStruct((1, 2, size * listed), F32),
        ),
        in_specs=[vmem] + [hbm] * 5,
        out_specs=(vmem, vmem),
        scratch_shapes=[
            pltpu.VMEM((size, size), F32),
            pltpu.VMEM((slabs, 2, size // 2 + 8, size // 2), F32),
            pltpu.VMEM((slabs, size, size), F32),
            pltpu.VMEM((points, 2, packed, LANES), F32),
            pltpu.VMEM((2, size, size), F32),
            pltpu.VMEM((2, size, size), F32),
            pltpu.VMEM((2, size, LANES), F32),
            pltpu.VMEM((2, size, LANES), jnp.int32),
            pltpu.VMEM((size, size), jnp.int32),
            pltpu.VMEM((2, listed, size), jnp.int32),
            pltpu.SMEM(propagator.shape, F32),
            dma((5,)),
            dma((slabs, 2)),
            dma((slabs, 2, 2)),
            dma((slabs, 2)),
            dma((points // 2,)),
            dma((points,)),
            dma((points // 2,)),
            dma,
        ],
        compiler_params=pltpu.CompilerParams(
            collective_id=0, has_side_effects=True, vmem_limit_bytes=60 * 1024 * 1024
        ),
        cost_estimate=pl.CostEstimate(
            flops=200 * size**3, bytes_accessed=8 * size * size * 4, transcendentals=0
        ),
    )(jnp.stack([energies, broadening], axis=1), hamiltonian, coupling, propagator, neighbors.T, phonon_modes.T)
    return green, part


def solution(mesh):
    return jax.shard_map(
        functools.partial(body, mesh.shape["slab"], mesh.shape["energy"]),
        mesh=mesh,
        in_specs=(
            P("energy"),
            P("energy"),
            P("slab", None),
            P("slab", None),
            P(),
            P("slab", None),
            P("slab", None),
        ),
        out_specs=(P("energy", None, "slab", None), P("energy", None, "slab")),
        check_vma=False,
    )
```

```python
import functools
import math

import jax
import jax.numpy as jnp
from jax import lax
from jax.experimental import pallas as pl
from jax.experimental.pallas import tpu as pltpu
from jax.sharding import PartitionSpec as P

F32 = jnp.float32
BF16 = jnp.bfloat16
MESH = pl.DeviceIdType.MESH
LANES = 128


def split(x):
    hi = x.astype(BF16)
    return hi, (x - hi.astype(F32)).astype(BF16)


def dot3(a, b, transposed=False):
    dims = (((1,), (1 if transposed else 0,)), ((), ()))
    dot = functools.partial(lax.dot_general, dimension_numbers=dims, preferred_element_type=F32)
    return dot(a[0], b[0]) + (dot(a[0], b[1]) + dot(a[1], b[0]))


def triple(re, im):
    return split(re), split(im), split(re + im)


def product(a, b):
    first, second, mixed = (dot3(x, y) for x, y in zip(a, b))
    return first - second, mixed - first - second


def take(values, index):
    return jnp.take_along_axis(values, index, axis=1, mode="promise_in_bounds")


def kernel(
    slabs, points, scale,
    shift_ref, h_hbm, c_hbm, k_hbm, nbr_hbm, mode_hbm,
    green_ref, self_ref,
    h_ref, hp, cb, pg, s_ref, g_ref, rep, irep, inv_ref, lists, k_ref,
    local, send1, recv1, fwd1, send2, recv2, fwd2, twin_send,
):
    size = h_ref.shape[0]
    listed = nbr_hbm.shape[0]
    modes = k_ref.shape[1]
    groups = LANES // listed
    packed_rows = size // groups
    chunks = size // LANES
    chips = points // 2
    me_slab, me = lax.axis_index("slab"), lax.axis_index("energy")
    par, chip = lax.rem(me, 2), lax.div(me, 2)
    twin = me + 1 - 2 * par

    loads = [
        pltpu.make_async_copy(source, target, local.at[n])
        for n, (source, target) in enumerate(
            (
                (h_hbm, h_ref),
                (nbr_hbm, lists.at[0]),
                (mode_hbm, lists.at[1]),
                (c_hbm, cb.at[me_slab]),
                (k_hbm, k_ref),
            )
        )
    ]
    for load in loads:
        load.start()

    barrier = pltpu.get_barrier_semaphore()

    def greet(slab, point):
        pl.semaphore_signal(barrier, inc=1, device_id=(slab, point), device_id_type=MESH)

    for d in range(1, slabs):
        greet(lax.rem(me_slab + d, slabs), me)
    greet(me_slab, twin)
    for d in range(1, chips):
        greet(me_slab, lax.rem(chip + d, chips) * 2 + par)
    half_rows = size // 2

    def half(which):
        return pl.ds(pl.multiple_of(which * half_rows, half_rows), half_rows)

    def place(b, item, which):
        return hp.at[b, which] if item == 0 else cb.at[b, half(which)]

    def block_copy(target, item):
        return pltpu.make_async_remote_copy(
            src_ref=hp.at[me_slab, par] if item == 0 else c_hbm.at[half(par)],
            dst_ref=place(me_slab, item, par),
            send_sem=send1.at[target, item],
            recv_sem=recv1.at[me_slab, item, par],
            device_id=(target, me),
            device_id_type=MESH,
        )

    def block_forward(b, item, which):
        return pltpu.make_async_remote_copy(
            src_ref=place(b, item, which), dst_ref=place(b, item, which),
            send_sem=fwd1.at[b, item], recv_sem=recv1.at[b, item, which],
            device_id=(me_slab, twin), device_id_type=MESH,
        )

    small_row = lax.broadcasted_iota(jnp.int32, (half_rows, half_rows), 0)
    small_col = lax.broadcasted_iota(jnp.int32, (half_rows, half_rows), 1)
    loads[0].wait()
    first = h_ref[:half_rows, :half_rows]
    last = h_ref[half_rows:, half_rows:]
    hp[me_slab, 0, :half_rows] = jnp.where(small_row <= small_col, first, last)
    ends = jnp.sum(jnp.where(small_row == small_col, last, 0.0), axis=0, keepdims=True)
    hp[me_slab, 0, half_rows:] = jnp.broadcast_to(ends, (8, half_rows))
    hp[me_slab, 1, :half_rows] = h_ref[:half_rows, half_rows:]
    hp[me_slab, 1, half_rows:] = jnp.zeros((8, half_rows), F32)

    pl.semaphore_wait(barrier, slabs - 1 + 1 + chips - 1)

    for target in reversed(range(1, slabs)):
        @pl.when(target > me_slab)
        def _():
            block_copy(target, 0).start()

    for target in reversed(range(1, slabs)):
        @pl.when(jnp.logical_and(target > me_slab, me_slab > 0))
        def _():
            block_copy(target, 1).start()

    def hamiltonian_block(b):
        square = hp[b, 0, :half_rows]
        turned = square.T
        corner = hp[b, 1, :half_rows]
        ends = hp[b, 0, half_rows : half_rows + 1]
        first = jnp.where(small_row <= small_col, square, turned)
        last = jnp.where(small_row > small_col, square, turned)
        last = jnp.where(small_row == small_col, ends, last)
        top = jnp.concatenate([first, corner], axis=1)
        bottom = jnp.concatenate([corner.T, last], axis=1)
        return jnp.concatenate([top, bottom], axis=0)

    for load in loads[1:]:
        load.wait()

    row = lax.broadcasted_iota(jnp.int32, (size, size), 0)
    col = lax.broadcasted_iota(jnp.int32, (size, size), 1)
    eye = row == col

    irep[0] = jnp.concatenate([lists[0].T] * groups, axis=1)
    irep[1] = jnp.concatenate([lists[1].T] * groups, axis=1)

    column = lax.broadcasted_iota(jnp.int32, (size, size), 1)
    inv = jnp.full((size, size), -1, jnp.int32)
    for k in range(listed):
        inv = jnp.where(irep[0, :, k : k + 1] == column, k, inv)
    inv_ref[...] = inv

    group = lax.broadcasted_iota(jnp.int32, (packed_rows, LANES), 1) // listed

    def pack(ref):
        out = ref[pl.ds(0, packed_rows, stride=groups), :]
        for q in range(1, groups):
            out = jnp.where(group == q, ref[pl.ds(q, packed_rows, stride=groups), :], out)
        return out

    def refine(b, through):
        s_re = jnp.where(eye, shift_ref[:, :1], 0.0) - hamiltonian_block(b)
        s_im = jnp.where(eye, shift_ref[:, 1:], 0.0)
        if through is not None:
            s_re, s_im = s_re - through[0], s_im - through[1]
        s_ref[0] = s_re
        s_ref[1] = s_im
        diag_re = jnp.where(eye, s_re, 0.0)
        diag_im = jnp.where(eye, s_im, 0.0)

        def reciprocal(axis):
            re = jnp.sum(diag_re, axis=axis, keepdims=True)
            im = jnp.sum(diag_im, axis=axis, keepdims=True)
            modulus = re * re + im * im
            return re / modulus, -im / modulus

        di_re, di_im = reciprocal(1)
        dj_re, dj_im = reciprocal(0)
        o_re = di_re * dj_re - di_im * dj_im
        o_im = di_re * dj_im + di_im * dj_re
        x_re = jnp.where(eye, 2.0 * di_re, 0.0) - (o_re * s_re - o_im * s_im)
        x_im = jnp.where(eye, 2.0 * di_im, 0.0) - (o_re * s_im + o_im * s_re)
        x = triple(x_re, x_im)
        p_re, p_im = product(triple(s_re, s_im), x)
        out_re, out_im = product(x, triple(jnp.where(eye, 2.0, 0.0) - p_re, -p_im))
        g_ref[0] = out_re
        g_ref[1] = out_im

    def pass_on(b, items):
        copies = [block_forward(b, item, par) for item in items]
        for copy in copies:
            copy.wait_recv()
            copy.start()

    def arrive(b, items):
        for item in items:
            block_forward(b, item, 1 - par).wait_recv()

    @pl.when(me_slab > 0)
    def _():
        pass_on(0, (0,))
        arrive(0, (0,))

    refine(0, None)

    def pass_on_later(b, carry):
        pass_on(b, (0, 1))
        return carry

    lax.fori_loop(1, me_slab, pass_on_later, 0)

    def step(b, carry):
        @pl.when(b < me_slab)
        def _():
            arrive(b, (0, 1))

        c = split(cb[b])
        through = [dot3(split(dot3(c, split(g_ref[i]))), c, transposed=True) for i in range(2)]
        refine(b, through)
        return carry

    lax.fori_loop(1, me_slab + 1, step, 0)

    for i in range(2):
        index = irep[0]
        values = take(g_ref[i, :, :LANES], index & (LANES - 1))
        for chunk in range(1, chunks):
            part = take(g_ref[i, :, chunk * LANES : (chunk + 1) * LANES], index & (LANES - 1))
            values = jnp.where(index >= chunk * LANES, part, values)
        rep[i] = values
        pg[me, i] = pack(rep.at[i])

    def pair_copy(d):
        other = lax.rem(chip + d, chips)
        return pltpu.make_async_remote_copy(
            src_ref=pg.at[me], dst_ref=pg.at[me],
            send_sem=send2.at[d], recv_sem=recv2.at[me],
            device_id=(me_slab, other * 2 + par), device_id_type=MESH,
        )

    def pair_forward(d, which):
        point = lax.rem(chip + d, chips) * 2 + which
        return pltpu.make_async_remote_copy(
            src_ref=pg.at[point], dst_ref=pg.at[point],
            send_sem=fwd2.at[d], recv_sem=recv2.at[point],
            device_id=(me_slab, twin), device_id_type=MESH,
        )

    def own_forward(point):
        return pltpu.make_async_remote_copy(
            src_ref=pg.at[point], dst_ref=pg.at[point],
            send_sem=twin_send, recv_sem=recv2.at[point],
            device_id=(me_slab, twin), device_id_type=MESH,
        )

    def each(first, last, act):
        lax.fori_loop(first, last, lambda d, carry: (act(d), carry)[1], 0)

    each(1, chips, lambda d: pair_copy(d).start())
    own_forward(me).start()

    g = triple(g_ref[0], g_ref[1])
    p_re, p_im = product(triple(s_ref[0], s_ref[1]), g)
    e_re, e_im = product(g, triple(jnp.where(eye, 2.0, 0.0) - p_re, -p_im))
    green_ref[0, 0] = e_re
    green_ref[0, 1] = e_im

    mode = pack(irep.at[1])
    nbr = pack(irep.at[0])

    def add_point(point, total):
        k_re = jnp.zeros((packed_rows, LANES), F32)
        k_im = jnp.zeros((packed_rows, LANES), F32)
        for m in range(modes):
            k_re = jnp.where(mode == m, k_ref[0, m, me, point], k_re)
            k_im = jnp.where(mode == m, k_ref[1, m, me, point], k_im)
        v_re, v_im = pg[point, 0], pg[point, 1]
        return total[0] + (k_re * v_re - k_im * v_im), total[1] + (k_re * v_im + k_im * v_re)

    zero = jnp.zeros((packed_rows, LANES), F32)
    total = add_point(me, (zero, zero))
    own_forward(twin).wait_recv()
    total = add_point(twin, total)

    def near(d, total):
        copy = pair_forward(d, par)
        copy.wait_recv()
        copy.start()
        return add_point(lax.rem(chip + d, chips) * 2 + par, total)

    def far(d, total):
        pair_forward(d, 1 - par).wait_recv()
        return add_point(lax.rem(chip + d, chips) * 2 + 1 - par, total)

    total = lax.fori_loop(1, chips, near, total)
    total = lax.fori_loop(1, chips, far, total)
    part = [scale * t for t in total]
    for line in range(packed_rows):
        self_ref[0, :, line * LANES : (line + 1) * LANES] = jnp.concatenate(
            [p[line : line + 1] for p in part], axis=0
        )

    lane = lax.broadcasted_iota(jnp.int32, (packed_rows, LANES), 1)
    start = lane - lax.rem(lane, listed)
    summed = list(part)
    for d in range(1, listed):
        index = start + lax.rem(lane + d, listed)
        same = take(nbr, index) == nbr
        for i in range(2):
            summed[i] = summed[i] + jnp.where(same, take(part[i], index), 0.0)
    offset = lax.rem(lax.broadcasted_iota(jnp.int32, (size, LANES), 0), groups) * listed
    sigma = []
    for i in range(2):
        for q in range(groups):
            rep[i, pl.ds(q, packed_rows, stride=groups), :] = summed[i]
        values = rep[i]
        pieces = []
        for chunk in range(chunks):
            where = inv_ref[:, chunk * LANES : (chunk + 1) * LANES]
            pieces.append(
                jnp.where(where >= 0, take(values, offset + jnp.maximum(where, 0)), 0.0)
            )
        sigma.append(jnp.concatenate(pieces, axis=1))
    g = triple(g_ref[0], g_ref[1])
    p_re, p_im = product(triple(*sigma), g)
    f_re, f_im = product(g, triple(p_re, p_im))
    green_ref[0, 0] = green_ref[0, 0] + f_re
    green_ref[0, 1] = green_ref[0, 1] + f_im

    for target in range(1, slabs):
        @pl.when(target > me_slab)
        def _():
            block_copy(target, 0).wait_send()

            @pl.when(me_slab > 0)
            def _():
                block_copy(target, 1).wait_send()

    for b in range(slabs):
        @pl.when(b < me_slab)
        def _():
            for item in ((0,) if b == 0 else (0, 1)):
                block_forward(b, item, par).wait_send()

    each(1, chips, lambda d: pair_copy(d).wait_send())
    each(1, chips, lambda d: pair_forward(d, par).wait_send())
    own_forward(me).wait_send()


def body(slabs, points, energies, broadening, hamiltonian, coupling, propagator, neighbors, phonon_modes):
    assert energies.shape[0] == 1 and points % 2 == 0
    size, listed = neighbors.shape
    scale = 2.0 * math.sqrt(size / listed)
    packed = size * listed // LANES
    hbm = pl.BlockSpec(memory_space=pltpu.HBM)
    vmem = pl.BlockSpec(memory_space=pltpu.VMEM)
    dma = pltpu.SemaphoreType.DMA
    operands = [
        pltpu.with_memory_space_constraint(x, pltpu.HBM)
        for x in (hamiltonian, coupling, propagator, neighbors.T, phonon_modes.T)
    ]
    green, part = pl.pallas_call(
        functools.partial(kernel, slabs, points, scale),
        out_shape=(
            jax.ShapeDtypeStruct((1, 2, size, size), F32),
            jax.ShapeDtypeStruct((1, 2, size * listed), F32),
        ),
        in_specs=[vmem] + [hbm] * 5,
        out_specs=(vmem, vmem),
        scratch_shapes=[
            pltpu.VMEM((size, size), F32),
            pltpu.VMEM((slabs, 2, size // 2 + 8, size // 2), F32),
            pltpu.VMEM((slabs, size, size), F32),
            pltpu.VMEM((points, 2, packed, LANES), F32),
            pltpu.VMEM((2, size, size), F32),
            pltpu.VMEM((2, size, size), F32),
            pltpu.VMEM((2, size, LANES), F32),
            pltpu.VMEM((2, size, LANES), jnp.int32),
            pltpu.VMEM((size, size), jnp.int32),
            pltpu.VMEM((2, listed, size), jnp.int32),
            pltpu.SMEM(propagator.shape, F32),
            dma((5,)),
            dma((slabs, 2)),
            dma((slabs, 2, 2)),
            dma((slabs, 2)),
            dma((points // 2,)),
            dma((points,)),
            dma((points // 2,)),
            dma,
        ],
        compiler_params=pltpu.CompilerParams(
            collective_id=0, has_side_effects=True, vmem_limit_bytes=40 * 1024 * 1024
        ),
        cost_estimate=pl.CostEstimate(
            flops=200 * size**3, bytes_accessed=8 * size * size * 4, transcendentals=0
        ),
    )(jnp.stack([energies, broadening], axis=1), *operands)
    return green, part


def solution(mesh):
    return jax.shard_map(
        functools.partial(body, mesh.shape["slab"], mesh.shape["energy"]),
        mesh=mesh,
        in_specs=(
            P("energy"),
            P("energy"),
            P("slab", None),
            P("slab", None),
            P(),
            P("slab", None),
            P("slab", None),
        ),
        out_specs=(P("energy", None, "slab", None), P("energy", None, "slab")),
        check_vma=False,
    )
```

```python
import functools
import math

import jax
import jax.numpy as jnp
from jax import lax
from jax.experimental import pallas as pl
from jax.experimental.pallas import tpu as pltpu
from jax.sharding import PartitionSpec as P

F32 = jnp.float32
BF16 = jnp.bfloat16
MESH = pl.DeviceIdType.MESH
LANES = 128


def split(x):
    hi = x.astype(BF16)
    return hi, (x - hi.astype(F32)).astype(BF16)


def dot3(a, b, transposed=False):
    dims = (((1,), (1 if transposed else 0,)), ((), ()))
    dot = functools.partial(lax.dot_general, dimension_numbers=dims, preferred_element_type=F32)
    return dot(a[0], b[0]) + (dot(a[0], b[1]) + dot(a[1], b[0]))


def triple(re, im):
    return split(re), split(im), split(re + im)


def product(a, b):
    first, second, mixed = (dot3(x, y) for x, y in zip(a, b))
    return first - second, mixed - first - second


def take(values, index):
    return jnp.take_along_axis(values, index, axis=1, mode="promise_in_bounds")


def kernel(
    slabs, points, scale,
    shift_ref, h_hbm, c_hbm, k_hbm, nbr_hbm, mode_hbm,
    green_ref, self_ref,
    h_ref, hp, cb, pg, s_ref, g_ref, rep, irep, inv_ref, lists, same, total, k_ref,
    local, send1, recv1, fwd1, send2, recv2, fwd2, twin_send,
):
    size = h_ref.shape[0]
    listed = nbr_hbm.shape[0]
    modes = k_ref.shape[1]
    groups = LANES // listed
    packed_rows = size // groups
    chunks = size // LANES
    chips = points // 2
    me_slab, me = lax.axis_index("slab"), lax.axis_index("energy")
    par, chip = lax.rem(me, 2), lax.div(me, 2)
    twin = me + 1 - 2 * par

    loads = [
        pltpu.make_async_copy(source, target, local.at[n])
        for n, (source, target) in enumerate(
            (
                (h_hbm, h_ref),
                (nbr_hbm, lists.at[0]),
                (mode_hbm, lists.at[1]),
                (c_hbm, cb.at[me_slab]),
                (k_hbm, k_ref),
            )
        )
    ]
    for load in loads:
        load.start()

    barrier = pltpu.get_barrier_semaphore()

    def greet(slab, point):
        pl.semaphore_signal(barrier, inc=1, device_id=(slab, point), device_id_type=MESH)

    for d in range(1, slabs):
        greet(lax.rem(me_slab + d, slabs), me)
    greet(me_slab, twin)
    for d in range(1, chips):
        greet(me_slab, lax.rem(chip + d, chips) * 2 + par)
    half_rows = size // 2

    def half(which):
        return pl.ds(pl.multiple_of(which * half_rows, half_rows), half_rows)

    def place(b, item, which):
        return hp.at[b, which] if item == 0 else cb.at[b, half(which)]

    def block_copy(target, item):
        return pltpu.make_async_remote_copy(
            src_ref=hp.at[me_slab, par] if item == 0 else c_hbm.at[half(par)],
            dst_ref=place(me_slab, item, par),
            send_sem=send1.at[target, item],
            recv_sem=recv1.at[me_slab, item, par],
            device_id=(target, me),
            device_id_type=MESH,
        )

    def block_forward(b, item, which):
        return pltpu.make_async_remote_copy(
            src_ref=place(b, item, which), dst_ref=place(b, item, which),
            send_sem=fwd1.at[b, item], recv_sem=recv1.at[b, item, which],
            device_id=(me_slab, twin), device_id_type=MESH,
        )

    small_row = lax.broadcasted_iota(jnp.int32, (half_rows, half_rows), 0)
    small_col = lax.broadcasted_iota(jnp.int32, (half_rows, half_rows), 1)
    loads[0].wait()
    first = h_ref[:half_rows, :half_rows]
    last = h_ref[half_rows:, half_rows:]
    hp[me_slab, 0, :half_rows] = jnp.where(small_row <= small_col, first, last)
    ends = jnp.sum(jnp.where(small_row == small_col, last, 0.0), axis=0, keepdims=True)
    hp[me_slab, 0, half_rows:] = jnp.broadcast_to(ends, (8, half_rows))
    hp[me_slab, 1, :half_rows] = h_ref[:half_rows, half_rows:]
    hp[me_slab, 1, half_rows:] = jnp.zeros((8, half_rows), F32)

    pl.semaphore_wait(barrier, slabs - 1 + 1 + chips - 1)

    for target in reversed(range(1, slabs)):
        @pl.when(target > me_slab)
        def _():
            block_copy(target, 0).start()

    for target in range(1, slabs):
        @pl.when(jnp.logical_and(target > me_slab, me_slab > 0))
        def _():
            block_copy(target, 1).start()

    def hamiltonian_block(b):
        square = hp[b, 0, :half_rows]
        turned = square.T
        corner = hp[b, 1, :half_rows]
        ends = hp[b, 0, half_rows : half_rows + 1]
        first = jnp.where(small_row <= small_col, square, turned)
        last = jnp.where(small_row > small_col, square, turned)
        last = jnp.where(small_row == small_col, ends, last)
        top = jnp.concatenate([first, corner], axis=1)
        bottom = jnp.concatenate([corner.T, last], axis=1)
        return jnp.concatenate([top, bottom], axis=0)

    for load in loads[1:]:
        load.wait()

    row = lax.broadcasted_iota(jnp.int32, (size, size), 0)
    col = lax.broadcasted_iota(jnp.int32, (size, size), 1)
    eye = row == col

    irep[0] = jnp.concatenate([lists[0].T] * groups, axis=1)
    irep[1] = jnp.concatenate([lists[1].T] * groups, axis=1)

    column = lax.broadcasted_iota(jnp.int32, (size, size), 1)
    inv = jnp.full((size, size), -1, jnp.int32)
    for k in range(listed):
        inv = jnp.where(irep[0, :, k : k + 1] == column, k, inv)
    inv_ref[...] = inv

    group = lax.broadcasted_iota(jnp.int32, (packed_rows, LANES), 1) // listed

    def pack(ref):
        out = ref[pl.ds(0, packed_rows, stride=groups), :]
        for q in range(1, groups):
            out = jnp.where(group == q, ref[pl.ds(q, packed_rows, stride=groups), :], out)
        return out

    def refine(b, through):
        s_re = jnp.where(eye, shift_ref[:, :1], 0.0) - hamiltonian_block(b)
        s_im = jnp.where(eye, shift_ref[:, 1:], 0.0)
        if through is not None:
            s_re, s_im = s_re - through[0], s_im - through[1]
        s_ref[0] = s_re
        s_ref[1] = s_im
        diag_re = jnp.where(eye, s_re, 0.0)
        diag_im = jnp.where(eye, s_im, 0.0)

        def reciprocal(axis):
            re = jnp.sum(diag_re, axis=axis, keepdims=True)
            im = jnp.sum(diag_im, axis=axis, keepdims=True)
            modulus = re * re + im * im
            return re / modulus, -im / modulus

        di_re, di_im = reciprocal(1)
        dj_re, dj_im = reciprocal(0)
        o_re = di_re * dj_re - di_im * dj_im
        o_im = di_re * dj_im + di_im * dj_re
        x_re = jnp.where(eye, 2.0 * di_re, 0.0) - (o_re * s_re - o_im * s_im)
        x_im = jnp.where(eye, 2.0 * di_im, 0.0) - (o_re * s_im + o_im * s_re)
        x = triple(x_re, x_im)
        p_re, p_im = product(triple(s_re, s_im), x)
        out_re, out_im = product(x, triple(jnp.where(eye, 2.0, 0.0) - p_re, -p_im))
        g_ref[0] = out_re
        g_ref[1] = out_im

    def pass_on(b, items):
        copies = [block_forward(b, item, par) for item in items]
        for copy in copies:
            copy.wait_recv()
            copy.start()

    def arrive(b, items):
        for item in items:
            block_forward(b, item, 1 - par).wait_recv()

    @pl.when(me_slab > 0)
    def _():
        pass_on(0, (0,))
        arrive(0, (0,))

    refine(0, None)

    def pass_on_later(b, carry):
        pass_on(b, (0, 1))
        return carry

    lax.fori_loop(1, me_slab, pass_on_later, 0)

    def step(b, carry):
        @pl.when(b < me_slab)
        def _():
            arrive(b, (0, 1))

        c = split(cb[b])
        through = [dot3(split(dot3(c, split(g_ref[i]))), c, transposed=True) for i in range(2)]
        refine(b, through)
        return carry

    lax.fori_loop(1, me_slab + 1, step, 0)

    for i in range(2):
        index = irep[0]
        values = take(g_ref[i, :, :LANES], index & (LANES - 1))
        for chunk in range(1, chunks):
            part = take(g_ref[i, :, chunk * LANES : (chunk + 1) * LANES], index & (LANES - 1))
            values = jnp.where(index >= chunk * LANES, part, values)
        rep[i] = values
        pg[me, i] = pack(rep.at[i])

    def pair_copy(other):
        return pltpu.make_async_remote_copy(
            src_ref=pg.at[me], dst_ref=pg.at[me],
            send_sem=send2.at[other], recv_sem=recv2.at[me],
            device_id=(me_slab, other * 2 + par), device_id_type=MESH,
        )

    def pair_forward(other, which):
        point = other * 2 + which
        return pltpu.make_async_remote_copy(
            src_ref=pg.at[point], dst_ref=pg.at[point],
            send_sem=fwd2.at[other], recv_sem=recv2.at[point],
            device_id=(me_slab, twin), device_id_type=MESH,
        )

    def own_forward(point):
        return pltpu.make_async_remote_copy(
            src_ref=pg.at[point], dst_ref=pg.at[point],
            send_sem=twin_send, recv_sem=recv2.at[point],
            device_id=(me_slab, twin), device_id_type=MESH,
        )

    def partners(distances, act):
        for distance in distances:
            @pl.when(chip >= distance)
            def _():
                act(chip - distance)

            @pl.when(chip + distance < chips)
            def _():
                act(chip + distance)

    partners(reversed(range(1, chips)), lambda other: pair_copy(other).start())
    own_forward(me).start()

    g = triple(g_ref[0], g_ref[1])
    p_re, p_im = product(triple(s_ref[0], s_ref[1]), g)
    e_re, e_im = product(g, triple(jnp.where(eye, 2.0, 0.0) - p_re, -p_im))
    green_ref[0, 0] = e_re
    green_ref[0, 1] = e_im

    mode = pack(irep.at[1])
    nbr = pack(irep.at[0])

    lane = lax.broadcasted_iota(jnp.int32, (packed_rows, LANES), 1)
    start = lane - lax.rem(lane, listed)

    def turned_lanes(d):
        return start + lax.rem(lane + d, listed)

    for d in range(1, listed):
        same[d] = jnp.where(take(nbr, turned_lanes(d)) == nbr, 1.0, 0.0)

    total[...] = jnp.zeros_like(total)

    def add_point(point):
        k_re = jnp.zeros((packed_rows, LANES), F32)
        k_im = jnp.zeros((packed_rows, LANES), F32)
        for m in range(modes):
            k_re = jnp.where(mode == m, k_ref[0, m, me, point], k_re)
            k_im = jnp.where(mode == m, k_ref[1, m, me, point], k_im)
        v_re, v_im = pg[point, 0], pg[point, 1]
        total[0] = total[0] + (k_re * v_re - k_im * v_im)
        total[1] = total[1] + (k_re * v_im + k_im * v_re)

    def near(other):
        copy = pair_forward(other, par)
        copy.wait_recv()
        copy.start()
        add_point(other * 2 + par)

    def far(other):
        pair_forward(other, 1 - par).wait_recv()
        add_point(other * 2 + 1 - par)

    add_point(me)
    own_forward(twin).wait_recv()
    add_point(twin)
    partners(range(1, chips), near)
    partners(range(1, chips), far)
    part = [scale * total[i] for i in range(2)]
    for line in range(packed_rows):
        self_ref[0, :, line * LANES : (line + 1) * LANES] = jnp.concatenate(
            [p[line : line + 1] for p in part], axis=0
        )

    summed = list(part)
    for d in range(1, listed):
        for i in range(2):
            summed[i] = summed[i] + same[d] * take(part[i], turned_lanes(d))
    offset = lax.rem(lax.broadcasted_iota(jnp.int32, (size, LANES), 0), groups) * listed
    sigma = []
    for i in range(2):
        for q in range(groups):
            rep[i, pl.ds(q, packed_rows, stride=groups), :] = summed[i]
        values = rep[i]
        pieces = []
        for chunk in range(chunks):
            where = inv_ref[:, chunk * LANES : (chunk + 1) * LANES]
            pieces.append(
                jnp.where(where >= 0, take(values, offset + jnp.maximum(where, 0)), 0.0)
            )
        sigma.append(jnp.concatenate(pieces, axis=1))
    g = triple(g_ref[0], g_ref[1])
    p_re, p_im = product(triple(*sigma), g)
    f_re, f_im = product(g, triple(p_re, p_im))
    green_ref[0, 0] = green_ref[0, 0] + f_re
    green_ref[0, 1] = green_ref[0, 1] + f_im

    for target in range(1, slabs):
        @pl.when(target > me_slab)
        def _():
            block_copy(target, 0).wait_send()

            @pl.when(me_slab > 0)
            def _():
                block_copy(target, 1).wait_send()

    for b in range(slabs):
        @pl.when(b < me_slab)
        def _():
            for item in ((0,) if b == 0 else (0, 1)):
                block_forward(b, item, par).wait_send()

    partners(range(1, chips), lambda other: pair_copy(other).wait_send())
    partners(range(1, chips), lambda other: pair_forward(other, par).wait_send())
    own_forward(me).wait_send()


def body(slabs, points, energies, broadening, hamiltonian, coupling, propagator, neighbors, phonon_modes):
    assert energies.shape[0] == 1 and points % 2 == 0
    size, listed = neighbors.shape
    scale = 2.0 * math.sqrt(size / listed)
    packed = size * listed // LANES
    hbm = pl.BlockSpec(memory_space=pltpu.HBM)
    vmem = pl.BlockSpec(memory_space=pltpu.VMEM)
    dma = pltpu.SemaphoreType.DMA
    operands = [
        pltpu.with_memory_space_constraint(x, pltpu.HBM)
        for x in (hamiltonian, coupling, propagator, neighbors.T, phonon_modes.T)
    ]
    green, part = pl.pallas_call(
        functools.partial(kernel, slabs, points, scale),
        out_shape=(
            jax.ShapeDtypeStruct((1, 2, size, size), F32),
            jax.ShapeDtypeStruct((1, 2, size * listed), F32),
        ),
        in_specs=[vmem] + [hbm] * 5,
        out_specs=(vmem, vmem),
        scratch_shapes=[
            pltpu.VMEM((size, size), F32),
            pltpu.VMEM((slabs, 2, size // 2 + 8, size // 2), F32),
            pltpu.VMEM((slabs, size, size), F32),
            pltpu.VMEM((points, 2, packed, LANES), F32),
            pltpu.VMEM((2, size, size), F32),
            pltpu.VMEM((2, size, size), F32),
            pltpu.VMEM((2, size, LANES), F32),
            pltpu.VMEM((2, size, LANES), jnp.int32),
            pltpu.VMEM((size, size), jnp.int32),
            pltpu.VMEM((2, listed, size), jnp.int32),
            pltpu.VMEM((listed, packed, LANES), F32),
            pltpu.VMEM((2, packed, LANES), F32),
            pltpu.SMEM(propagator.shape, F32),
            dma((5,)),
            dma((slabs, 2)),
            dma((slabs, 2, 2)),
            dma((slabs, 2)),
            dma((points // 2,)),
            dma((points,)),
            dma((points // 2,)),
            dma,
        ],
        compiler_params=pltpu.CompilerParams(
            collective_id=0, has_side_effects=True, vmem_limit_bytes=40 * 1024 * 1024
        ),
        cost_estimate=pl.CostEstimate(
            flops=200 * size**3, bytes_accessed=8 * size * size * 4, transcendentals=0
        ),
    )(jnp.stack([energies, broadening], axis=1), *operands)
    return green, part


def solution(mesh):
    return jax.shard_map(
        functools.partial(body, mesh.shape["slab"], mesh.shape["energy"]),
        mesh=mesh,
        in_specs=(
            P("energy"),
            P("energy"),
            P("slab", None),
            P("slab", None),
            P(),
            P("slab", None),
            P("slab", None),
        ),
        out_specs=(P("energy", None, "slab", None), P("energy", None, "slab")),
        check_vma=False,
    )
```

```python
import functools
import math

import jax
import jax.numpy as jnp
from jax import lax
from jax.experimental import pallas as pl
from jax.experimental.pallas import tpu as pltpu
from jax.sharding import PartitionSpec as P

F32 = jnp.float32
BF16 = jnp.bfloat16
MESH = pl.DeviceIdType.MESH
LANES = 128


def split(x):
    hi = x.astype(BF16)
    return hi, (x - hi.astype(F32)).astype(BF16)


def dot3(a, b, transposed=False):
    dims = (((1,), (1 if transposed else 0,)), ((), ()))
    dot = functools.partial(lax.dot_general, dimension_numbers=dims, preferred_element_type=F32)
    return dot(a[0], b[0]) + (dot(a[0], b[1]) + dot(a[1], b[0]))


def triple(re, im):
    return split(re), split(im), split(re + im)


def product(a, b):
    first, second, mixed = (dot3(x, y) for x, y in zip(a, b))
    return first - second, mixed - first - second


def take(values, index):
    return jnp.take_along_axis(values, index, axis=1, mode="promise_in_bounds")


def kernel(
    slabs, points, scale,
    shift_ref, h_hbm, c_hbm, k_hbm, nbr_hbm, mode_hbm,
    green_ref, self_ref,
    h_ref, hp, cb, pg, s_ref, g_ref, rep, irep, inv_ref, lists, same, total, k_ref,
    local, send1, recv1, fwd1, send2, recv2, fwd2, twin_send,
):
    size = h_ref.shape[0]
    listed = nbr_hbm.shape[0]
    modes = k_ref.shape[1]
    groups = LANES // listed
    packed_rows = size // groups
    chunks = size // LANES
    chips = points // 2
    me_slab, me = lax.axis_index("slab"), lax.axis_index("energy")
    par, chip = lax.rem(me, 2), lax.div(me, 2)
    twin = me + 1 - 2 * par

    loads = [
        pltpu.make_async_copy(source, target, local.at[n])
        for n, (source, target) in enumerate(
            (
                (h_hbm, h_ref),
                (nbr_hbm, lists.at[0]),
                (mode_hbm, lists.at[1]),
                (c_hbm, cb.at[me_slab]),
                (k_hbm, k_ref),
            )
        )
    ]
    for load in loads:
        load.start()

    barrier = pltpu.get_barrier_semaphore()

    def greet(slab, point):
        pl.semaphore_signal(barrier, inc=1, device_id=(slab, point), device_id_type=MESH)

    for d in range(1, slabs):
        greet(lax.rem(me_slab + d, slabs), me)
    greet(me_slab, twin)
    for d in range(1, chips):
        greet(me_slab, lax.rem(chip + d, chips) * 2 + par)
    half_rows = size // 2

    def half(which):
        return pl.ds(pl.multiple_of(which * half_rows, half_rows), half_rows)

    def place(b, item, which):
        return hp.at[b, which] if item == 0 else cb.at[b, half(which)]

    def block_copy(target, item):
        return pltpu.make_async_remote_copy(
            src_ref=hp.at[me_slab, par] if item == 0 else c_hbm.at[half(par)],
            dst_ref=place(me_slab, item, par),
            send_sem=send1.at[target, item],
            recv_sem=recv1.at[me_slab, item, par],
            device_id=(target, me),
            device_id_type=MESH,
        )

    def block_forward(b, item, which):
        return pltpu.make_async_remote_copy(
            src_ref=place(b, item, which), dst_ref=place(b, item, which),
            send_sem=fwd1.at[b, item], recv_sem=recv1.at[b, item, which],
            device_id=(me_slab, twin), device_id_type=MESH,
        )

    small_row = lax.broadcasted_iota(jnp.int32, (half_rows, half_rows), 0)
    small_col = lax.broadcasted_iota(jnp.int32, (half_rows, half_rows), 1)
    loads[0].wait()
    first = h_ref[:half_rows, :half_rows]
    last = h_ref[half_rows:, half_rows:]
    hp[me_slab, 0, :half_rows] = jnp.where(small_row <= small_col, first, last)
    ends = jnp.sum(jnp.where(small_row == small_col, last, 0.0), axis=0, keepdims=True)
    hp[me_slab, 0, half_rows:] = jnp.broadcast_to(ends, (8, half_rows))
    hp[me_slab, 1, :half_rows] = h_ref[:half_rows, half_rows:]
    hp[me_slab, 1, half_rows:] = jnp.zeros((8, half_rows), F32)

    pl.semaphore_wait(barrier, slabs - 1 + 1 + chips - 1)

    for target in reversed(range(1, slabs)):
        @pl.when(target > me_slab)
        def _():
            block_copy(target, 0).start()

    for target in range(1, slabs):
        @pl.when(jnp.logical_and(target > me_slab, me_slab > 0))
        def _():
            block_copy(target, 1).start()

    def hamiltonian_block(b):
        square = hp[b, 0, :half_rows]
        turned = square.T
        corner = hp[b, 1, :half_rows]
        ends = hp[b, 0, half_rows : half_rows + 1]
        first = jnp.where(small_row <= small_col, square, turned)
        last = jnp.where(small_row > small_col, square, turned)
        last = jnp.where(small_row == small_col, ends, last)
        top = jnp.concatenate([first, corner], axis=1)
        bottom = jnp.concatenate([corner.T, last], axis=1)
        return jnp.concatenate([top, bottom], axis=0)

    for load in loads[1:3]:
        load.wait()

    row = lax.broadcasted_iota(jnp.int32, (size, size), 0)
    col = lax.broadcasted_iota(jnp.int32, (size, size), 1)
    eye = row == col

    irep[0] = jnp.concatenate([lists[0].T] * groups, axis=1)
    irep[1] = jnp.concatenate([lists[1].T] * groups, axis=1)

    column = lax.broadcasted_iota(jnp.int32, (size, size), 1)
    inv = jnp.full((size, size), -1, jnp.int32)
    for k in range(listed):
        inv = jnp.where(irep[0, :, k : k + 1] == column, k, inv)
    inv_ref[...] = inv

    group = lax.broadcasted_iota(jnp.int32, (packed_rows, LANES), 1) // listed

    def pack(ref):
        out = ref[pl.ds(0, packed_rows, stride=groups), :]
        for q in range(1, groups):
            out = jnp.where(group == q, ref[pl.ds(q, packed_rows, stride=groups), :], out)
        return out

    def refine(b, through):
        s_re = jnp.where(eye, shift_ref[:, :1], 0.0) - hamiltonian_block(b)
        s_im = jnp.where(eye, shift_ref[:, 1:], 0.0)
        if through is not None:
            s_re, s_im = s_re - through[0], s_im - through[1]
        s_ref[0] = s_re
        s_ref[1] = s_im
        diag_re = jnp.where(eye, s_re, 0.0)
        diag_im = jnp.where(eye, s_im, 0.0)

        def reciprocal(axis):
            re = jnp.sum(diag_re, axis=axis, keepdims=True)
            im = jnp.sum(diag_im, axis=axis, keepdims=True)
            modulus = re * re + im * im
            return re / modulus, -im / modulus

        di_re, di_im = reciprocal(1)
        dj_re, dj_im = reciprocal(0)
        o_re = di_re * dj_re - di_im * dj_im
        o_im = di_re * dj_im + di_im * dj_re
        x_re = jnp.where(eye, 2.0 * di_re, 0.0) - (o_re * s_re - o_im * s_im)
        x_im = jnp.where(eye, 2.0 * di_im, 0.0) - (o_re * s_im + o_im * s_re)
        x = triple(x_re, x_im)
        p_re, p_im = product(triple(s_re, s_im), x)
        out_re, out_im = product(x, triple(jnp.where(eye, 2.0, 0.0) - p_re, -p_im))
        g_ref[0] = out_re
        g_ref[1] = out_im

    def pass_on(b, items):
        copies = [block_forward(b, item, par) for item in items]
        for copy in copies:
            copy.wait_recv()
            copy.start()

    def arrive(b, items):
        for item in items:
            block_forward(b, item, 1 - par).wait_recv()

    @pl.when(me_slab > 0)
    def _():
        pass_on(0, (0,))
        arrive(0, (0,))

    refine(0, None)

    def pass_on_later(b, carry):
        pass_on(b, (0, 1))
        return carry

    lax.fori_loop(1, me_slab, pass_on_later, 0)
    loads[3].wait()

    def step(b, carry):
        @pl.when(b < me_slab)
        def _():
            arrive(b, (0, 1))

        c = split(cb[b])
        through = [dot3(split(dot3(c, split(g_ref[i]))), c, transposed=True) for i in range(2)]
        refine(b, through)
        return carry

    lax.fori_loop(1, me_slab + 1, step, 0)

    for i in range(2):
        index = irep[0]
        values = take(g_ref[i, :, :LANES], index & (LANES - 1))
        for chunk in range(1, chunks):
            part = take(g_ref[i, :, chunk * LANES : (chunk + 1) * LANES], index & (LANES - 1))
            values = jnp.where(index >= chunk * LANES, part, values)
        rep[i] = values
        pg[me, i] = pack(rep.at[i])

    def pair_copy(other):
        return pltpu.make_async_remote_copy(
            src_ref=pg.at[me], dst_ref=pg.at[me],
            send_sem=send2.at[other], recv_sem=recv2.at[me],
            device_id=(me_slab, other * 2 + par), device_id_type=MESH,
        )

    def pair_forward(other, which):
        point = other * 2 + which
        return pltpu.make_async_remote_copy(
            src_ref=pg.at[point], dst_ref=pg.at[point],
            send_sem=fwd2.at[other], recv_sem=recv2.at[point],
            device_id=(me_slab, twin), device_id_type=MESH,
        )

    def own_forward(point):
        return pltpu.make_async_remote_copy(
            src_ref=pg.at[point], dst_ref=pg.at[point],
            send_sem=twin_send, recv_sem=recv2.at[point],
            device_id=(me_slab, twin), device_id_type=MESH,
        )

    def partners(distances, act):
        for distance in distances:
            @pl.when(chip >= distance)
            def _():
                act(chip - distance)

            @pl.when(chip + distance < chips)
            def _():
                act(chip + distance)

    partners(reversed(range(1, chips)), lambda other: pair_copy(other).start())
    own_forward(me).start()

    g = triple(g_ref[0], g_ref[1])
    p_re, p_im = product(triple(s_ref[0], s_ref[1]), g)
    e_re, e_im = product(g, triple(jnp.where(eye, 2.0, 0.0) - p_re, -p_im))
    green_ref[0, 0] = e_re
    green_ref[0, 1] = e_im

    mode = pack(irep.at[1])
    nbr = pack(irep.at[0])

    lane = lax.broadcasted_iota(jnp.int32, (packed_rows, LANES), 1)
    start = lane - lax.rem(lane, listed)

    def turned_lanes(d):
        return start + lax.rem(lane + d, listed)

    for d in range(1, listed):
        same[d] = jnp.where(take(nbr, turned_lanes(d)) == nbr, 1.0, 0.0)

    total[...] = jnp.zeros_like(total)

    def add_point(point):
        k_re = jnp.zeros((packed_rows, LANES), F32)
        k_im = jnp.zeros((packed_rows, LANES), F32)
        for m in range(modes):
            k_re = jnp.where(mode == m, k_ref[0, m, me, point], k_re)
            k_im = jnp.where(mode == m, k_ref[1, m, me, point], k_im)
        v_re, v_im = pg[point, 0], pg[point, 1]
        total[0] = total[0] + (k_re * v_re - k_im * v_im)
        total[1] = total[1] + (k_re * v_im + k_im * v_re)

    def near(other):
        copy = pair_forward(other, par)
        copy.wait_recv()
        copy.start()
        add_point(other * 2 + par)

    def far(other):
        pair_forward(other, 1 - par).wait_recv()
        add_point(other * 2 + 1 - par)

    loads[4].wait()
    add_point(me)
    own_forward(twin).wait_recv()
    add_point(twin)
    partners(range(1, chips), near)
    partners(range(1, chips), far)
    part = [scale * total[i] for i in range(2)]
    for line in range(packed_rows):
        self_ref[0, :, line * LANES : (line + 1) * LANES] = jnp.concatenate(
            [p[line : line + 1] for p in part], axis=0
        )

    summed = list(part)
    for d in range(1, listed):
        for i in range(2):
            summed[i] = summed[i] + same[d] * take(part[i], turned_lanes(d))
    offset = lax.rem(lax.broadcasted_iota(jnp.int32, (size, LANES), 0), groups) * listed
    sigma = []
    for i in range(2):
        for q in range(groups):
            rep[i, pl.ds(q, packed_rows, stride=groups), :] = summed[i]
        values = rep[i]
        pieces = []
        for chunk in range(chunks):
            where = inv_ref[:, chunk * LANES : (chunk + 1) * LANES]
            pieces.append(
                jnp.where(where >= 0, take(values, offset + jnp.maximum(where, 0)), 0.0)
            )
        sigma.append(jnp.concatenate(pieces, axis=1))
    g = triple(g_ref[0], g_ref[1])
    p_re, p_im = product(triple(*sigma), g)
    f_re, f_im = product(g, triple(p_re, p_im))
    green_ref[0, 0] = green_ref[0, 0] + f_re
    green_ref[0, 1] = green_ref[0, 1] + f_im

    for target in range(1, slabs):
        @pl.when(target > me_slab)
        def _():
            block_copy(target, 0).wait_send()

            @pl.when(me_slab > 0)
            def _():
                block_copy(target, 1).wait_send()

    for b in range(slabs):
        @pl.when(b < me_slab)
        def _():
            for item in ((0,) if b == 0 else (0, 1)):
                block_forward(b, item, par).wait_send()

    partners(range(1, chips), lambda other: pair_copy(other).wait_send())
    partners(range(1, chips), lambda other: pair_forward(other, par).wait_send())
    own_forward(me).wait_send()


def body(slabs, points, energies, broadening, hamiltonian, coupling, propagator, neighbors, phonon_modes):
    assert energies.shape[0] == 1 and points % 2 == 0
    size, listed = neighbors.shape
    scale = 2.0 * math.sqrt(size / listed)
    packed = size * listed // LANES
    hbm = pl.BlockSpec(memory_space=pltpu.HBM)
    vmem = pl.BlockSpec(memory_space=pltpu.VMEM)
    dma = pltpu.SemaphoreType.DMA
    operands = [
        pltpu.with_memory_space_constraint(x, pltpu.HBM)
        for x in (hamiltonian, coupling, propagator, neighbors.T, phonon_modes.T)
    ]
    green, part = pl.pallas_call(
        functools.partial(kernel, slabs, points, scale),
        out_shape=(
            jax.ShapeDtypeStruct((1, 2, size, size), F32),
            jax.ShapeDtypeStruct((1, 2, size * listed), F32),
        ),
        in_specs=[vmem] + [hbm] * 5,
        out_specs=(vmem, vmem),
        scratch_shapes=[
            pltpu.VMEM((size, size), F32),
            pltpu.VMEM((slabs, 2, size // 2 + 8, size // 2), F32),
            pltpu.VMEM((slabs, size, size), F32),
            pltpu.VMEM((points, 2, packed, LANES), F32),
            pltpu.VMEM((2, size, size), F32),
            pltpu.VMEM((2, size, size), F32),
            pltpu.VMEM((2, size, LANES), F32),
            pltpu.VMEM((2, size, LANES), jnp.int32),
            pltpu.VMEM((size, size), jnp.int32),
            pltpu.VMEM((2, listed, size), jnp.int32),
            pltpu.VMEM((listed, packed, LANES), F32),
            pltpu.VMEM((2, packed, LANES), F32),
            pltpu.SMEM(propagator.shape, F32),
            dma((5,)),
            dma((slabs, 2)),
            dma((slabs, 2, 2)),
            dma((slabs, 2)),
            dma((points // 2,)),
            dma((points,)),
            dma((points // 2,)),
            dma,
        ],
        compiler_params=pltpu.CompilerParams(
            collective_id=0, has_side_effects=True, vmem_limit_bytes=40 * 1024 * 1024
        ),
        cost_estimate=pl.CostEstimate(
            flops=200 * size**3, bytes_accessed=8 * size * size * 4, transcendentals=0
        ),
    )(jnp.stack([energies, broadening], axis=1), *operands)
    return green, part


def solution(mesh):
    return jax.shard_map(
        functools.partial(body, mesh.shape["slab"], mesh.shape["energy"]),
        mesh=mesh,
        in_specs=(
            P("energy"),
            P("energy"),
            P("slab", None),
            P("slab", None),
            P(),
            P("slab", None),
            P("slab", None),
        ),
        out_specs=(P("energy", None, "slab", None), P("energy", None, "slab")),
        check_vma=False,
    )
```
